256 devices in a mesh: section: 8 (over z_lo, core), ctx: 32 (over y, z_hi, x).
Axes of the slice: x: 4, y: 4, z: 8 (z_hi: 2, z_lo: 4; z = z_hi * 4 + z_lo), core: 2. Of those that a mesh axis runs over, the one named last changes fastest.
Arguments:
- sent_queries: bfloat16 [8, 4096, 4096], P('section', 'ctx'), may hold values from -60 to 60
- sent_keyvals: bfloat16 [8, 4096, 2, 512], P('section', 'ctx'), may hold values from -5 to 5
- forward_lengths: int32 [8, 16], P('section'), may hold values from 1 to 512, 4096 in all within a row
- kept_queries: bfloat16 [8, 4096, 4096], P('section', 'ctx'), may hold values from -60 to 60
- kept_keyvals: bfloat16 [8, 4096, 2, 512], P('section', 'ctx'), may hold values from -5 to 5
- sent_grad: bfloat16 [8, 4096, 4096], P('section', 'ctx'), may hold values from -6 to 6
- backward_lengths: int32 [8, 16], P('section'), may hold values from 1 to 512, 4096 in all within a row
Outputs:
- attention_out: bfloat16 [8, 4096, 4096], P('section', 'ctx')
- query_grad: bfloat16 [8, 4096, 4096], P('section', 'ctx')
- keyval_grad: bfloat16 [8, 4096, 2, 512], P('section', 'ctx')
The draws below stay inside these ranges and needn't reach their ends.
Inputs may be any that keep to these rules, and one draw needn't show every extreme that they name: `forward_lengths`: each row of 16 lengths sums to 4096; the longest document has exactly 512 tokens. `backward_lengths`: each row of 16 lengths sums to 4096; the longest document has exactly 512 tokens.
All inputs are finite; a program needn't handle non-finite values.
Results may differ from the reference program's by a relative error of at most 0.04.
Values may be sent and summed in bfloat16 or wider, within the bound.
No kernel may reach another device: no remote copies, remote signals or barrier semaphores. Data moves between devices by JAX's collectives and lax.ppermute only.
A program may use at most 128 MiB of HBM per device.

```python
import math
import jax
import jax.numpy as jnp
import numpy as np
from jax import lax

QUERY_HEADS = 32
LOCAL_KV_HEADS = 4
HEAD_WIDTH = 128
TOKENS_PER_SHARD = 128
DOCS = 16
MOST = 512
SEQUENCE_TOKENS = 4096
RELAY_SECTIONS = 8
QUERY_WIDTH = 4096
KVW = 512
N_CTX = 32


def pair_draw(key, salt_value, aligned):
    key = jax.random.fold_in(key, salt_value)
    sub_keys = jax.random.split(key, 5)
    normal_queries = jnp.clip(jax.random.normal(sub_keys[0], (RELAY_SECTIONS, SEQUENCE_TOKENS, QUERY_WIDTH), jnp.float32), -5.0, 5.0)
    normal_keyvals = jnp.clip(jax.random.normal(sub_keys[2], (RELAY_SECTIONS, SEQUENCE_TOKENS, 2, KVW), jnp.float32), -5.0, 5.0)
    query_heads_input = normal_queries
    keyvals = normal_keyvals
    strength = jax.random.uniform(sub_keys[4], (RELAY_SECTIONS, SEQUENCE_TOKENS, 1), jnp.float32, 10.0, 30.0)
    positions = jnp.arange(SEQUENCE_TOKENS, dtype=jnp.int32)
    chosen = (positions % 64 == 63).astype(jnp.float32)[None, :, None] * aligned
    key_matrix = keyvals[:, :, 0, :]
    query_heads_input = query_heads_input * (1.0 - chosen)
    shrink = 1.0 - 0.18 / strength
    chosen_before = jnp.roll(chosen, -1, axis=1)
    keys_before = jnp.roll(key_matrix * shrink, -1, axis=1)
    key_matrix = key_matrix * (1.0 - chosen_before) + chosen_before * keys_before
    keyvals = jnp.stack([key_matrix, keyvals[:, :, 1, :]], axis=2)
    return (query_heads_input, keyvals)


def draw_sent_queries(key, part):
    aligned = 0.0
    return pair_draw(key, 5, aligned)[0].astype(jnp.bfloat16)


def draw_sent_keyvals(key, part):
    aligned = 0.0
    return pair_draw(key, 5, aligned)[1].astype(jnp.bfloat16)


def draw_kept_queries(key, part):
    aligned = 0.0
    return pair_draw(key, 9, aligned)[0].astype(jnp.bfloat16)


def draw_kept_keyvals(key, part):
    aligned = 0.0
    return pair_draw(key, 9, aligned)[1].astype(jnp.bfloat16)


def steps_of(own_key, shape, cuts, smallest, high):
    def one(axis_at, shards_of):
        heights = jax.random.uniform(jax.random.fold_in(jax.random.fold_in(own_key, 6), axis_at), (shards_of,), jnp.float32, smallest / len(cuts), high / len(cuts))
        return jnp.repeat(jnp.exp(heights), shape[axis_at] // shards_of).reshape((-1,) + (1,) * (len(shape) - axis_at - 1))

    level = one(*cuts[0])
    for cut in cuts[1:]:
        level = level * one(*cut)
    return level


def profile(count, total, limit, slope):
    loads = [(1 << 20) // math.isqrt(standing ** slope) + 1 for standing in range(2, count + 1)]
    rest, counts = total - limit - (count - 1), [1] * (count - 1)
    while rest > 0:
        free = [i for i in range(count - 1) if counts[i] < limit]
        mass, budget = sum([loads[i] for i in free]), rest
        for i in free:
            more = min(limit - counts[i], max(1, budget * loads[i] // mass), rest)
            counts[i] = counts[i] + more
            rest = rest - more
    return np.array([limit] + counts)


def uneven(rng, amount, total, reach, skew):
    if amount == 2:
        one = jax.random.randint(rng, (), max(1, total - reach), min(reach, total - 1) + 1)
        return jnp.stack([one, total - one])
    sizes = jnp.asarray(profile(amount, total, reach, skew), jnp.int32)
    twos = (amount - 1) // 2
    source_of, receiver = sizes[1:1 + 2 * twos:2], sizes[2:2 + 2 * twos:2]
    margin = jnp.minimum(source_of - 1, reach - receiver)
    passed = jax.random.randint(jax.random.fold_in(rng, 1), (twos,), 0, 1 << 20) % (margin + 1)
    sizes = sizes.at[1:1 + 2 * twos:2].set(source_of - passed).at[2:2 + 2 * twos:2].set(receiver + passed)
    return sizes[jax.random.permutation(jax.random.fold_in(rng, 2), amount)]


def centred(rng, dims, deviation, reach, cuts=(), held_as=jnp.bfloat16):
    result = deviation * jax.random.normal(rng, dims, jnp.float32)
    if cuts:
        result = result * steps_of(rng, dims, cuts, -0.22, 0.18)
    return jnp.clip(result, -reach, reach).astype(held_as)


def setup_inputs(seed: int = 0) -> dict:
    seeds = jax.random.split(jax.random.key(seed), 8)
    return {
        "sent_queries": draw_sent_queries(jax.random.fold_in(seeds[7], 71), 0),
        "sent_keyvals": draw_sent_keyvals(jax.random.fold_in(seeds[7], 71), 0),
        "forward_lengths": jax.vmap(lambda own: uneven(own, DOCS, SEQUENCE_TOKENS, MOST, 2))(jax.random.split(seeds[2], RELAY_SECTIONS)).reshape((RELAY_SECTIONS, DOCS)).astype(jnp.int32),
        "kept_queries": draw_kept_queries(jax.random.fold_in(seeds[7], 71), 0),
        "kept_keyvals": draw_kept_keyvals(jax.random.fold_in(seeds[7], 71), 0),
        "sent_grad": centred(seeds[5], (RELAY_SECTIONS, SEQUENCE_TOKENS, QUERY_WIDTH), 1.0, 6.0, ((0, 8), (1, 32))),
        "backward_lengths": jax.vmap(lambda own: uneven(own, DOCS, SEQUENCE_TOKENS, MOST, 2))(jax.random.split(seeds[6], RELAY_SECTIONS)).reshape((RELAY_SECTIONS, DOCS)).astype(jnp.int32),
    }


masked_value = -1e+30

def rounded_output(values):
    return lax.optimization_barrier(values.astype(jnp.bfloat16)).astype(jnp.float32)

def document_of(lengths, positions):
    doc_ends = jnp.cumsum(lengths)
    return lax.optimization_barrier(jnp.sum((positions[:, None] >= doc_ends[None, :]).astype(jnp.int32), axis=1))

def window_terms(query_matrix, key_window, lengths, first_row):
    group_count = QUERY_HEADS // LOCAL_KV_HEADS
    window_length = MOST + TOKENS_PER_SHARD
    logit_scale = 1.0 / math.sqrt(HEAD_WIDTH)
    query_heads_input = query_matrix.reshape(TOKENS_PER_SHARD, LOCAL_KV_HEADS, group_count, HEAD_WIDTH).astype(jnp.float32)
    key_matrix = key_window[:, 0].reshape(window_length, LOCAL_KV_HEADS, HEAD_WIDTH).astype(jnp.float32)
    value_matrix = key_window[:, 1].reshape(window_length, LOCAL_KV_HEADS, HEAD_WIDTH).astype(jnp.float32)
    query_pos = first_row + jnp.arange(TOKENS_PER_SHARD, dtype=jnp.int32)
    key_pos = first_row - MOST + jnp.arange(window_length, dtype=jnp.int32)
    same_doc = document_of(lengths, query_pos)[:, None] == document_of(lengths, key_pos)[None, :]
    allowed = same_doc & (key_pos[None, :] <= query_pos[:, None]) & (key_pos[None, :] >= 0)
    attention_scores = jnp.einsum('wofu,aou->ofwa', query_heads_input, key_matrix, precision=lax.Precision.HIGHEST) * logit_scale
    attention_scores = jnp.where(allowed, attention_scores, masked_value)
    row_top = lax.optimization_barrier(jnp.max(attention_scores, axis=-1))
    exponent_weights = jnp.where(allowed, jnp.exp(attention_scores - row_top[..., None]), 0.0)
    row_total = lax.optimization_barrier(jnp.sum(exponent_weights, axis=-1))
    weighted_values = jnp.einsum('qmoe,eqx->qmox', rounded_output(exponent_weights), value_matrix, precision=lax.Precision.HIGHEST)
    attended_rows = (weighted_values / row_total[..., None]).transpose(2, 0, 1, 3).reshape(TOKENS_PER_SHARD, QUERY_WIDTH).astype(jnp.bfloat16)
    return (query_heads_input, key_matrix, value_matrix, allowed, attention_scores, row_top + jnp.log(row_total), attended_rows)

def padded_keys(keyvals):
    return jnp.concatenate([jnp.zeros((MOST, 2, KVW), keyvals.dtype), keyvals], axis=0)

def forward_section(section_items):
    query_all, keyval_all, lengths = section_items
    padded = padded_keys(keyval_all)

    def one_shard(shard_index):
        first_row = (shard_index * TOKENS_PER_SHARD).astype(jnp.int32)
        query_matrix = lax.dynamic_slice_in_dim(query_all, first_row, TOKENS_PER_SHARD, 0)
        key_window = lax.dynamic_slice_in_dim(padded, first_row, MOST + TOKENS_PER_SHARD, 0)
        return window_terms(query_matrix, key_window, lengths, first_row)[6]
    return lax.map(one_shard, jnp.arange(N_CTX, dtype=jnp.int32)).reshape(SEQUENCE_TOKENS, QUERY_WIDTH)

def backward_section(section_items):
    query_all, keyval_all, grad_all, lengths = section_items
    padded = padded_keys(keyval_all)
    group_count = QUERY_HEADS // LOCAL_KV_HEADS
    logit_scale = 1.0 / math.sqrt(HEAD_WIDTH)

    def one_shard(accum, shard_index):
        first_row = (shard_index * TOKENS_PER_SHARD).astype(jnp.int32)
        query_matrix = lax.dynamic_slice_in_dim(query_all, first_row, TOKENS_PER_SHARD, 0)
        gradient_rows = lax.dynamic_slice_in_dim(grad_all, first_row, TOKENS_PER_SHARD, 0)
        key_window = lax.dynamic_slice_in_dim(padded, first_row, MOST + TOKENS_PER_SHARD, 0)
        query_heads_input, key_matrix, value_matrix, allowed, attention_scores, log_total, attended_rows = window_terms(query_matrix, key_window, lengths, first_row)
        incoming_gradient = gradient_rows.reshape(TOKENS_PER_SHARD, LOCAL_KV_HEADS, group_count, HEAD_WIDTH).astype(jnp.float32)
        recompute_forward = attended_rows.reshape(TOKENS_PER_SHARD, LOCAL_KV_HEADS, group_count, HEAD_WIDTH).astype(jnp.float32)
        delta_rows = lax.optimization_barrier(jnp.sum(incoming_gradient * recompute_forward, axis=-1)).transpose(1, 2, 0)
        softmax_probabilities = jnp.where(allowed, jnp.exp(attention_scores - log_total[..., None]), 0.0)
        value_gradients = jnp.einsum('cvby,bcvi->yci', rounded_output(softmax_probabilities), incoming_gradient, precision=lax.Precision.HIGHEST)
        probability_gradients = jnp.einsum('wofu,aou->ofwa', incoming_gradient, value_matrix, precision=lax.Precision.HIGHEST)
        score_gradients = rounded_output(softmax_probabilities * (probability_gradients - delta_rows[..., None]))
        query_gradients = jnp.einsum('oqbh,hou->boqu', score_gradients, key_matrix, precision=lax.Precision.HIGHEST) * logit_scale
        key_gradients = jnp.einsum('cvby,bcvi->yci', score_gradients, query_heads_input, precision=lax.Precision.HIGHEST) * logit_scale
        parts = rounded_output(jnp.stack([key_gradients, value_gradients], axis=1).reshape(MOST + TOKENS_PER_SHARD, 2, KVW))
        current = lax.dynamic_slice_in_dim(accum, first_row, MOST + TOKENS_PER_SHARD, 0)
        accum = lax.dynamic_update_slice_in_dim(accum, current + parts, first_row, 0)
        return (accum, query_gradients.reshape(TOKENS_PER_SHARD, QUERY_WIDTH).astype(jnp.bfloat16))
    accum, query_gradients = lax.scan(one_shard, jnp.zeros((SEQUENCE_TOKENS + MOST, 2, KVW), jnp.float32), jnp.arange(N_CTX, dtype=jnp.int32))
    return (query_gradients.reshape(SEQUENCE_TOKENS, QUERY_WIDTH), accum[MOST:].astype(jnp.bfloat16))

def reference(sent_queries, sent_keyvals, forward_lengths, kept_queries, kept_keyvals, sent_grad, backward_lengths):
    arrived_queries = jnp.roll(sent_queries, 1, axis=0)
    arrived_keyvals = jnp.roll(sent_keyvals, 1, axis=0)
    incoming_gradient = jnp.roll(sent_grad, -1, axis=0)
    attention_out = lax.map(forward_section, (arrived_queries, arrived_keyvals, forward_lengths))
    query_grad, keyval_grad = lax.map(backward_section, (kept_queries, kept_keyvals, incoming_gradient, backward_lengths))
    return (attention_out, query_grad, keyval_grad)
```

```python
import math

import jax
import jax.numpy as jnp
from jax import lax
from jax.experimental import pallas as pl
from jax.experimental.pallas import tpu as pltpu
from jax.sharding import PartitionSpec as P

QUERY_HEADS = 32
KV_HEADS = 4
GROUP = QUERY_HEADS // KV_HEADS
WIDTH = 128
REACH = 4
ROW = 4
LOGIT_SCALE = 1.0 / math.sqrt(WIDTH)
EXP2_SCALE = LOGIT_SCALE * math.log2(math.e)
MASKED = -1e30
CHUNK_HEADS = 2

SMEM = pl.BlockSpec(memory_space=pltpu.SMEM)


def along_section(block, distance):
    size = lax.axis_size("section")
    return lax.ppermute(
        block, "section", [(i, (i + distance) % size) for i in range(size)]
    )


def across_rows(block, distance):
    size = lax.axis_size("ctx")
    return lax.ppermute(
        block,
        "ctx",
        [(i, i + distance) for i in range(size) if 0 <= i + distance < size],
    )


def across_rows_and_section(block, distance):
    sections, size = lax.axis_size("section"), lax.axis_size("ctx")
    route = [
        (s * size + c, (s + 1) % sections * size + c + distance)
        for s in range(sections)
        for c in range(size)
        if 0 <= c + distance < size
    ]
    return lax.ppermute(block, ("section", "ctx"), route)


def in_row(block, distance):
    size = lax.axis_size("ctx")
    return lax.ppermute(
        block,
        "ctx",
        [(c, c // ROW * ROW + (c + distance) % ROW) for c in range(size)],
    )


def after(values, earlier):
    return lax.optimization_barrier((values, earlier))[0]


def nt_dot(a, b):
    return lax.dot_general(a, b, (((1,), (1,)), ((), ())), preferred_element_type=jnp.float32)


def nn_dot(a, b):
    return jnp.dot(a, b, preferred_element_type=jnp.float32)


def write_bias(lengths_ref, bias_ref):
    tokens = bias_ref.shape[1]
    first_row = lax.axis_index("ctx") * tokens
    query = first_row + lax.broadcasted_iota(jnp.int32, (1, tokens), 1)
    start = jnp.zeros((1, tokens), jnp.int32)
    end = jnp.int32(0)
    for k in range(lengths_ref.shape[1]):
        end = end + lengths_ref[0, k]
        start = jnp.where(query >= end, end, start)
    for b in range(REACH + 1):
        key = (
            first_row
            + (b - REACH) * tokens
            + lax.broadcasted_iota(jnp.int32, (tokens, tokens), 0)
        )
        allowed = (key >= start) & (key <= query)
        bias_ref[b * tokens : (b + 1) * tokens, :] = jnp.where(allowed, 0.0, MASKED)


def head_rows(ref, first, count):
    return jnp.concatenate(
        [ref[:, h * WIDTH : (h + 1) * WIDTH] for h in range(first, first + count)], axis=0
    )


def window(block_refs, index):
    return jnp.concatenate([ref[index] for ref in block_refs], axis=0)


def exponentials(keys, queries, bias_ref):
    scores = nt_dot(keys, queries) * EXP2_SCALE + jnp.concatenate(
        [bias_ref[...]] * CHUNK_HEADS, axis=1
    )
    return jnp.exp2(scores - jnp.max(scores, axis=0, keepdims=True))


def forward_kernel(lengths_ref, q_ref, *refs):
    block_refs, (out_ref, bias_ref) = refs[: REACH + 1], refs[REACH + 1 :]

    @pl.when(pl.program_id(0) == 0)
    def _():
        write_bias(lengths_ref, bias_ref)

    keys = window(block_refs, 0)
    values_t = window(block_refs, 1).T
    for first in range(0, GROUP, CHUNK_HEADS):
        e = exponentials(keys, head_rows(q_ref, first, CHUNK_HEADS), bias_ref)
        total = jnp.sum(e, axis=0, keepdims=True)
        out_t = nn_dot(values_t, e.astype(jnp.bfloat16)) / total
        for k in range(CHUNK_HEADS):
            at = (first + k) * WIDTH
            out_ref[:, at : at + WIDTH] = out_t[:, k * WIDTH : (k + 1) * WIDTH].T.astype(
                jnp.bfloat16
            )


def backward_kernel(lengths_ref, q_ref, g_ref, *refs):
    block_refs, refs = refs[: REACH + 1], refs[REACH + 1 :]
    dq_ref, refs = refs[0], refs[1:]
    grad_refs, (bias_ref, p_ref, ds_ref) = refs[: REACH + 1], refs[REACH + 1 :]
    tokens = q_ref.shape[0]

    @pl.when(pl.program_id(0) == 0)
    def _():
        write_bias(lengths_ref, bias_ref)

    keys = window(block_refs, 0)
    values = window(block_refs, 1)
    keys_t = keys.T
    for first in range(0, GROUP, CHUNK_HEADS):
        lanes = slice(first * tokens, (first + CHUNK_HEADS) * tokens)
        e = exponentials(keys, head_rows(q_ref, first, CHUNK_HEADS), bias_ref)
        prob_grad = nt_dot(values, head_rows(g_ref, first, CHUNK_HEADS))
        inverse = 1.0 / jnp.sum(e, axis=0, keepdims=True)
        delta = jnp.sum(e * prob_grad, axis=0, keepdims=True) * inverse
        probs = e * inverse
        p_ref[:, lanes] = probs.astype(jnp.bfloat16)
        score_grad = (probs * (prob_grad - delta)).astype(jnp.bfloat16)
        ds_ref[:, lanes] = score_grad
        dq_t = nn_dot(keys_t, score_grad) * LOGIT_SCALE
        for k in range(CHUNK_HEADS):
            at = (first + k) * WIDTH
            dq_ref[:, at : at + WIDTH] = dq_t[:, k * WIDTH : (k + 1) * WIDTH].T.astype(
                jnp.bfloat16
            )
    value_grad = nn_dot(p_ref[...], head_rows(g_ref, 0, GROUP))
    key_grad = nn_dot(ds_ref[...], head_rows(q_ref, 0, GROUP)) * LOGIT_SCALE
    for b, ref in enumerate(grad_refs):
        rows = slice(b * tokens, (b + 1) * tokens)
        ref[0] = key_grad[rows].astype(ref.dtype)
        ref[1] = value_grad[rows].astype(ref.dtype)


def specs(tokens):
    group_cols = pl.BlockSpec((tokens, GROUP * WIDTH), lambda g: (0, g))
    pair = pl.BlockSpec((2, tokens, WIDTH), lambda g: (0, 0, g))
    return group_cols, pair


def forward(lengths, queries, blocks):
    tokens, width = queries.shape
    group_cols, pair = specs(tokens)
    keys = (REACH + 1) * tokens
    return pl.pallas_call(
        forward_kernel,
        grid=(KV_HEADS,),
        in_specs=[SMEM, group_cols] + [pair] * len(blocks),
        out_specs=group_cols,
        out_shape=jax.ShapeDtypeStruct((tokens, width), jnp.bfloat16),
        scratch_shapes=[pltpu.VMEM((keys, tokens), jnp.float32)],
        compiler_params=pltpu.CompilerParams(vmem_limit_bytes=40 * 1024 * 1024),
        cost_estimate=pl.CostEstimate(
            flops=4 * tokens * keys * width, bytes_accessed=4 << 20, transcendentals=0
        ),
        name="forward",
    )(lengths, queries, *blocks)


def backward(lengths, queries, grads, blocks):
    tokens, width = queries.shape
    group_cols, pair = specs(tokens)
    keys = (REACH + 1) * tokens
    kinds = [jnp.float32] + [jnp.bfloat16] * (REACH - 1) + [jnp.float32]
    return pl.pallas_call(
        backward_kernel,
        grid=(KV_HEADS,),
        in_specs=[SMEM, group_cols, group_cols] + [pair] * len(blocks),
        out_specs=[group_cols] + [pair] * len(blocks),
        out_shape=[jax.ShapeDtypeStruct((tokens, width), jnp.bfloat16)]
        + [jax.ShapeDtypeStruct(blocks[0].shape, kind) for kind in kinds],
        scratch_shapes=[
            pltpu.VMEM((keys, tokens), jnp.float32),
            pltpu.VMEM((keys, GROUP * tokens), jnp.bfloat16),
            pltpu.VMEM((keys, GROUP * tokens), jnp.bfloat16),
        ],
        compiler_params=pltpu.CompilerParams(vmem_limit_bytes=40 * 1024 * 1024),
        cost_estimate=pl.CostEstimate(
            flops=10 * tokens * keys * width, bytes_accessed=8 << 20, transcendentals=0
        ),
        name="backward",
    )(lengths, queries, grads, *blocks)


def gather_window(own, previous):
    place = lax.axis_index("ctx") % ROW
    blocks = [own]
    for distance in range(1, ROW):
        sent = jnp.where(place + distance < ROW, own, previous)
        blocks.insert(0, in_row(sent, distance))
    return [previous] + blocks


def return_terms(terms):
    place = lax.axis_index("ctx") % ROW
    previous, own = terms[0], terms[REACH]
    for distance in range(1, ROW):
        back = in_row(terms[REACH - distance], -distance).astype(jnp.float32)
        here = place + distance < ROW
        own = own + jnp.where(here, back, 0.0)
        previous = previous + jnp.where(here, 0.0, back)
    crossed = across_rows(previous.astype(jnp.bfloat16), -ROW)
    return own, crossed


def body(
    sent_queries,
    sent_keyvals,
    forward_lengths,
    kept_queries,
    kept_keyvals,
    sent_grad,
    backward_lengths,
):
    kept = kept_keyvals[0].transpose(1, 0, 2)
    kept_previous = across_rows(kept, ROW)
    grads = along_section(sent_grad[0], -1)
    sent = sent_keyvals[0].transpose(1, 0, 2)
    sent, queries = after((sent, sent_queries[0]), kept_previous)
    arrived_previous = across_rows_and_section(sent, ROW)
    arrived = along_section(sent, 1)
    arrived_queries = along_section(queries, 1)

    kept_window = gather_window(kept, kept_previous)
    results = backward(backward_lengths, kept_queries[0], grads, kept_window)
    own, crossed = return_terms(results[1:])

    attention_out = forward(
        forward_lengths, arrived_queries, gather_window(arrived, arrived_previous)
    )
    keyval_grad = (own + crossed.astype(jnp.float32)).astype(jnp.bfloat16).transpose(1, 0, 2)
    return attention_out[None], results[0][None], keyval_grad[None]


def solution(mesh):
    placed = (
        P("section", "ctx", None),
        P("section", "ctx", None, None),
        P("section", None),
        P("section", "ctx", None),
        P("section", "ctx", None, None),
        P("section", "ctx", None),
        P("section", None),
    )
    return jax.shard_map(
        body,
        mesh=mesh,
        in_specs=placed,
        out_specs=(
            P("section", "ctx", None),
            P("section", "ctx", None),
            P("section", "ctx", None, None),
        ),
        check_vma=False,
    )
```

```python
import math

import jax
import jax.numpy as jnp
from jax import lax
from jax.experimental import pallas as pl
from jax.experimental.pallas import tpu as pltpu
from jax.sharding import PartitionSpec as P

QUERY_HEADS = 32
KV_HEADS = 4
GROUP = QUERY_HEADS // KV_HEADS
WIDTH = 128
REACH = 4
ROW = 4
LOGIT_SCALE = 1.0 / math.sqrt(WIDTH)
EXP2_SCALE = LOGIT_SCALE * math.log2(math.e)
MASKED = -1e30
CHUNK_HEADS = 8

SMEM = pl.BlockSpec(memory_space=pltpu.SMEM)


def along_section(block, distance):
    size = lax.axis_size("section")
    return lax.ppermute(
        block, "section", [(i, (i + distance) % size) for i in range(size)]
    )


def across_rows(block, distance):
    size = lax.axis_size("ctx")
    return lax.ppermute(
        block,
        "ctx",
        [(i, i + distance) for i in range(size) if 0 <= i + distance < size],
    )


def across_rows_and_section(block, distance):
    sections, size = lax.axis_size("section"), lax.axis_size("ctx")
    route = [
        (s * size + c, (s + 1) % sections * size + c + distance)
        for s in range(sections)
        for c in range(size)
        if 0 <= c + distance < size
    ]
    return lax.ppermute(block, ("section", "ctx"), route)


def in_row(block, distance):
    size = lax.axis_size("ctx")
    return lax.ppermute(
        block,
        "ctx",
        [(c, c // ROW * ROW + (c + distance) % ROW) for c in range(size)],
    )


def after(values, earlier):
    return lax.optimization_barrier((values, earlier))[0]


def nt_dot(a, b):
    return lax.dot_general(a, b, (((1,), (1,)), ((), ())), preferred_element_type=jnp.float32)


def nn_dot(a, b):
    return jnp.dot(a, b, preferred_element_type=jnp.float32)


def write_bias(lengths_ref, bias_ref):
    tokens = bias_ref.shape[1]
    first_row = lax.axis_index("ctx") * tokens
    query = first_row + lax.broadcasted_iota(jnp.int32, (1, tokens), 1)
    start = jnp.zeros((1, tokens), jnp.int32)
    end = jnp.int32(0)
    for k in range(lengths_ref.shape[1]):
        end = end + lengths_ref[0, k]
        start = jnp.where(query >= end, end, start)
    for b in range(REACH + 1):
        key = (
            first_row
            + (b - REACH) * tokens
            + lax.broadcasted_iota(jnp.int32, (tokens, tokens), 0)
        )
        allowed = (key >= start) & (key <= query)
        bias_ref[b * tokens : (b + 1) * tokens, :] = jnp.where(allowed, 0.0, MASKED)


def head_rows(ref, first, count):
    return jnp.concatenate(
        [ref[:, h * WIDTH : (h + 1) * WIDTH] for h in range(first, first + count)], axis=0
    )


def window(block_refs, index):
    return jnp.concatenate([ref[index] for ref in block_refs], axis=0)


def exponentials(keys, queries, bias_ref):
    scores = nt_dot(keys, queries) * EXP2_SCALE + jnp.concatenate(
        [bias_ref[...]] * CHUNK_HEADS, axis=1
    )
    return jnp.exp2(scores - jnp.max(scores, axis=0, keepdims=True))


def forward_kernel(lengths_ref, q_ref, *refs):
    block_refs, (out_ref, bias_ref) = refs[: REACH + 1], refs[REACH + 1 :]

    @pl.when(pl.program_id(0) == 0)
    def _():
        write_bias(lengths_ref, bias_ref)

    keys = window(block_refs, 0)
    values_t = window(block_refs, 1).T
    for first in range(0, GROUP, CHUNK_HEADS):
        e = exponentials(keys, head_rows(q_ref, first, CHUNK_HEADS), bias_ref)
        total = jnp.sum(e, axis=0, keepdims=True)
        out_t = nn_dot(values_t, e.astype(jnp.bfloat16)) / total
        for k in range(CHUNK_HEADS):
            at = (first + k) * WIDTH
            out_ref[:, at : at + WIDTH] = out_t[:, k * WIDTH : (k + 1) * WIDTH].T.astype(
                jnp.bfloat16
            )


def backward_kernel(lengths_ref, q_ref, g_ref, *refs):
    block_refs, refs = refs[: REACH + 1], refs[REACH + 1 :]
    dq_ref, refs = refs[0], refs[1:]
    grad_refs, (bias_ref, p_ref, ds_ref) = refs[: REACH + 1], refs[REACH + 1 :]
    tokens = q_ref.shape[0]

    @pl.when(pl.program_id(0) == 0)
    def _():
        write_bias(lengths_ref, bias_ref)

    keys = window(block_refs, 0)
    values = window(block_refs, 1)
    keys_t = keys.T
    for first in range(0, GROUP, CHUNK_HEADS):
        lanes = slice(first * tokens, (first + CHUNK_HEADS) * tokens)
        e = exponentials(keys, head_rows(q_ref, first, CHUNK_HEADS), bias_ref)
        prob_grad = nt_dot(values, head_rows(g_ref, first, CHUNK_HEADS))
        inverse = 1.0 / jnp.sum(e, axis=0, keepdims=True)
        delta = jnp.sum(e * prob_grad, axis=0, keepdims=True) * inverse
        probs = e * inverse
        p_ref[:, lanes] = probs.astype(jnp.bfloat16)
        score_grad = (probs * (prob_grad - delta)).astype(jnp.bfloat16)
        ds_ref[:, lanes] = score_grad
        dq_t = nn_dot(keys_t, score_grad) * LOGIT_SCALE
        for k in range(CHUNK_HEADS):
            at = (first + k) * WIDTH
            dq_ref[:, at : at + WIDTH] = dq_t[:, k * WIDTH : (k + 1) * WIDTH].T.astype(
                jnp.bfloat16
            )
    value_grad = nn_dot(p_ref[...], head_rows(g_ref, 0, GROUP))
    key_grad = nn_dot(ds_ref[...], head_rows(q_ref, 0, GROUP)) * LOGIT_SCALE
    for b, ref in enumerate(grad_refs):
        rows = slice(b * tokens, (b + 1) * tokens)
        ref[0] = key_grad[rows].astype(ref.dtype)
        ref[1] = value_grad[rows].astype(ref.dtype)


def specs(tokens):
    group_cols = pl.BlockSpec((tokens, GROUP * WIDTH), lambda g: (0, g))
    pair = pl.BlockSpec((2, tokens, WIDTH), lambda g: (0, 0, g))
    return group_cols, pair


def forward(lengths, queries, blocks):
    tokens, width = queries.shape
    group_cols, pair = specs(tokens)
    keys = (REACH + 1) * tokens
    return pl.pallas_call(
        forward_kernel,
        grid=(KV_HEADS,),
        in_specs=[SMEM, group_cols] + [pair] * len(blocks),
        out_specs=group_cols,
        out_shape=jax.ShapeDtypeStruct((tokens, width), jnp.bfloat16),
        scratch_shapes=[pltpu.VMEM((keys, tokens), jnp.float32)],
        compiler_params=pltpu.CompilerParams(vmem_limit_bytes=40 * 1024 * 1024),
        cost_estimate=pl.CostEstimate(
            flops=4 * tokens * keys * width, bytes_accessed=4 << 20, transcendentals=0
        ),
        name="forward",
    )(lengths, queries, *blocks)


def backward(lengths, queries, grads, blocks):
    tokens, width = queries.shape
    group_cols, pair = specs(tokens)
    keys = (REACH + 1) * tokens
    kinds = [jnp.float32] + [jnp.bfloat16] * (REACH - 1) + [jnp.float32]
    return pl.pallas_call(
        backward_kernel,
        grid=(KV_HEADS,),
        in_specs=[SMEM, group_cols, group_cols] + [pair] * len(blocks),
        out_specs=[group_cols] + [pair] * len(blocks),
        out_shape=[jax.ShapeDtypeStruct((tokens, width), jnp.bfloat16)]
        + [jax.ShapeDtypeStruct(blocks[0].shape, kind) for kind in kinds],
        scratch_shapes=[
            pltpu.VMEM((keys, tokens), jnp.float32),
            pltpu.VMEM((keys, GROUP * tokens), jnp.bfloat16),
            pltpu.VMEM((keys, GROUP * tokens), jnp.bfloat16),
        ],
        compiler_params=pltpu.CompilerParams(vmem_limit_bytes=40 * 1024 * 1024),
        cost_estimate=pl.CostEstimate(
            flops=10 * tokens * keys * width, bytes_accessed=8 << 20, transcendentals=0
        ),
        name="backward",
    )(lengths, queries, grads, *blocks)


def window_sends(own, previous):
    place = lax.axis_index("ctx") % ROW
    return [jnp.where(place + d < ROW, own, previous) for d in range(1, ROW)]


def gather_window(own, previous, sends):
    moved = [in_row(sent, d) for d, sent in enumerate(sends, 1)]
    return [previous] + moved[::-1] + [own]


def return_terms(terms, earlier):
    place = lax.axis_index("ctx") % ROW
    previous, own = after(terms[0], earlier), terms[REACH]
    for distance in range(1, ROW):
        back = in_row(terms[REACH - distance], -distance).astype(jnp.float32)
        here = place + distance < ROW
        own = own + jnp.where(here, back, 0.0)
        previous = previous + jnp.where(here, 0.0, back)
    crossed = across_rows(previous.astype(jnp.bfloat16), -ROW)
    return own, crossed


def body(
    sent_queries,
    sent_keyvals,
    forward_lengths,
    kept_queries,
    kept_keyvals,
    sent_grad,
    backward_lengths,
):
    kept = kept_keyvals[0].transpose(1, 0, 2)
    sent = sent_keyvals[0].transpose(1, 0, 2)
    sent, grads = after((sent, sent_grad[0]), kept)
    kept_previous = across_rows(kept, ROW)
    grads = along_section(grads, -1)
    arrived_previous = across_rows_and_section(sent, ROW)
    arrived = along_section(sent, 1)
    kept_sends = window_sends(kept, kept_previous)
    kept_window = gather_window(kept, kept_previous, kept_sends)
    arrived, arrived_previous = after((arrived, arrived_previous), (kept_window[1:REACH], grads))
    arrived_sends = window_sends(arrived, arrived_previous)
    arrived_queries = along_section(after(sent_queries[0], arrived_sends), 1)
    kept_rows = after(kept_queries[0], arrived_sends)
    arrived_window = gather_window(arrived, arrived_previous, arrived_sends)
    results = backward(backward_lengths, kept_rows, grads, kept_window)
    attention_out = forward(forward_lengths, arrived_queries, arrived_window)
    own, crossed = return_terms(results[1:], attention_out)
    keyval_grad = (own + crossed.astype(jnp.float32)).astype(jnp.bfloat16).transpose(1, 0, 2)
    return attention_out[None], results[0][None], keyval_grad[None]


def solution(mesh):
    placed = (
        P("section", "ctx", None),
        P("section", "ctx", None, None),
        P("section", None),
        P("section", "ctx", None),
        P("section", "ctx", None, None),
        P("section", "ctx", None),
        P("section", None),
    )
    return jax.shard_map(
        body,
        mesh=mesh,
        in_specs=placed,
        out_specs=(
            P("section", "ctx", None),
            P("section", "ctx", None),
            P("section", "ctx", None, None),
        ),
        check_vma=False,
    )
```

```python
import math

import jax
import jax.numpy as jnp
from jax import lax
from jax.experimental import pallas as pl
from jax.experimental.pallas import tpu as pltpu
from jax.sharding import PartitionSpec as P

QUERY_HEADS = 32
KV_HEADS = 4
GROUP = QUERY_HEADS // KV_HEADS
WIDTH = 128
REACH = 4
ROW = 4
LOGIT_SCALE = 1.0 / math.sqrt(WIDTH)
EXP2_SCALE = LOGIT_SCALE * math.log2(math.e)
MASKED = -1e30
CHUNK_HEADS = 2
STEP_GROUPS = 2

SMEM = pl.BlockSpec(memory_space=pltpu.SMEM)


def along_section(block, distance):
    size = lax.axis_size("section")
    return lax.ppermute(
        block, "section", [(i, (i + distance) % size) for i in range(size)]
    )


def across_rows(block, distance):
    size = lax.axis_size("ctx")
    return lax.ppermute(
        block,
        "ctx",
        [(i, i + distance) for i in range(size) if 0 <= i + distance < size],
    )


def across_rows_and_section(block, distance):
    sections, size = lax.axis_size("section"), lax.axis_size("ctx")
    route = [
        (s * size + c, (s + 1) % sections * size + c + distance)
        for s in range(sections)
        for c in range(size)
        if 0 <= c + distance < size
    ]
    return lax.ppermute(block, ("section", "ctx"), route)


def in_row(block, distance):
    size = lax.axis_size("ctx")
    return lax.ppermute(
        block,
        "ctx",
        [(c, c // ROW * ROW + (c + distance) % ROW) for c in range(size)],
    )


def after(values, earlier):
    return lax.optimization_barrier((values, earlier))[0]


def nt_dot(a, b):
    return lax.dot_general(a, b, (((1,), (1,)), ((), ())), preferred_element_type=jnp.float32)


def nn_dot(a, b):
    return jnp.dot(a, b, preferred_element_type=jnp.float32)


def write_bias(lengths_ref, bias_ref):
    tokens = bias_ref.shape[1]
    first_row = lax.axis_index("ctx") * tokens
    query = first_row + lax.broadcasted_iota(jnp.int32, (1, tokens), 1)
    start = jnp.zeros((1, tokens), jnp.int32)
    end = jnp.int32(0)
    for k in range(lengths_ref.shape[1]):
        end = end + lengths_ref[0, k]
        start = jnp.where(query >= end, end, start)
    for b in range(REACH + 1):
        key = (
            first_row
            + (b - REACH) * tokens
            + lax.broadcasted_iota(jnp.int32, (tokens, tokens), 0)
        )
        allowed = (key >= start) & (key <= query)
        bias_ref[b * tokens : (b + 1) * tokens, :] = jnp.where(allowed, 0.0, MASKED)


def head_rows(ref, first, count):
    return jnp.concatenate(
        [ref[:, h * WIDTH : (h + 1) * WIDTH] for h in range(first, first + count)], axis=0
    )


def window(block_refs, index, group):
    columns = slice(group * WIDTH, (group + 1) * WIDTH)
    return jnp.concatenate([ref[index, :, columns] for ref in block_refs], axis=0)


def write_heads(ref, first, count, transposed):
    for k in range(count):
        at = (first + k) * WIDTH
        ref[:, at : at + WIDTH] = transposed[:, k * WIDTH : (k + 1) * WIDTH].T.astype(ref.dtype)


def exponentials(scores, bias):
    scores = scores * EXP2_SCALE + bias
    return jnp.exp2(scores - jnp.max(scores, axis=0, keepdims=True))


def forward_kernel(lengths_ref, q_ref, *refs):
    block_refs, (out_ref, bias_ref) = refs[: REACH + 1], refs[REACH + 1 :]
    write_bias(lengths_ref, bias_ref)
    bias = jnp.concatenate([bias_ref[...]] * GROUP, axis=1)
    for group in range(KV_HEADS):
        queries = head_rows(q_ref, group * GROUP, GROUP)
        e = exponentials(nt_dot(window(block_refs, 0, group), queries), bias)
        total = jnp.sum(e, axis=0, keepdims=True)
        out_t = nn_dot(window(block_refs, 1, group).T, e.astype(jnp.bfloat16)) / total
        write_heads(out_ref, group * GROUP, GROUP, out_t)


def backward_kernel(lengths_ref, q_ref, g_ref, *refs):
    block_refs, refs = refs[: REACH + 1], refs[REACH + 1 :]
    dq_ref, *grad_refs, bias_ref = refs
    tokens = q_ref.shape[0]

    @pl.when(pl.program_id(0) == 0)
    def _():
        write_bias(lengths_ref, bias_ref)

    bias = jnp.concatenate([bias_ref[...]] * CHUNK_HEADS, axis=1)
    keys = [window(block_refs, 0, group) for group in range(STEP_GROUPS)]
    values = [window(block_refs, 1, group) for group in range(STEP_GROUPS)]
    keys_t = [k.T for k in keys]
    chunks = [
        (group, group * GROUP + first)
        for group in range(STEP_GROUPS)
        for first in range(0, GROUP, CHUNK_HEADS)
    ]

    def products(chunk):
        group, first = chunk
        queries = head_rows(q_ref, first, CHUNK_HEADS)
        grads = head_rows(g_ref, first, CHUNK_HEADS)
        return queries, grads, nt_dot(keys[group], queries), nt_dot(values[group], grads)

    def score_terms(scores, prob_grad):
        e = exponentials(scores, bias)
        inverse = 1.0 / jnp.sum(e, axis=0, keepdims=True)
        delta = jnp.sum(e * prob_grad, axis=0, keepdims=True) * inverse
        probs = e * inverse
        return probs.astype(jnp.bfloat16), (probs * (prob_grad - delta)).astype(jnp.bfloat16)

    totals = [None] * STEP_GROUPS

    def gradients(chunk, queries, grads, probs, score_grad):
        group, first = chunk
        dq_t = nn_dot(keys_t[group], score_grad) * LOGIT_SCALE
        write_heads(dq_ref, first, CHUNK_HEADS, dq_t)
        terms = (nn_dot(score_grad, queries), nn_dot(probs, grads))
        if totals[group] is not None:
            terms = tuple(a + b for a, b in zip(totals[group], terms))
        totals[group] = terms

    ready, waiting = products(chunks[0]), None
    for at, chunk in enumerate(chunks):
        upcoming = products(chunks[at + 1]) if at + 1 < len(chunks) else None
        queries, grads, scores, prob_grad = ready
        terms = score_terms(scores, prob_grad)
        if waiting is not None:
            gradients(*waiting)
        ready, waiting = upcoming, (chunk, queries, grads, *terms)
    gradients(*waiting)

    for group, (key_grad, value_grad) in enumerate(totals):
        columns = slice(group * WIDTH, (group + 1) * WIDTH)
        for b, ref in enumerate(grad_refs):
            rows = slice(b * tokens, (b + 1) * tokens)
            ref[0, :, columns] = (key_grad[rows] * LOGIT_SCALE).astype(ref.dtype)
            ref[1, :, columns] = value_grad[rows].astype(ref.dtype)


def specs(tokens, groups):
    group_cols = pl.BlockSpec((tokens, groups * GROUP * WIDTH), lambda g: (0, g))
    pair = pl.BlockSpec((2, tokens, groups * WIDTH), lambda g: (0, 0, g))
    return group_cols, pair


def forward(lengths, queries, blocks):
    tokens, width = queries.shape
    group_cols, pair = specs(tokens, KV_HEADS)
    keys = (REACH + 1) * tokens
    return pl.pallas_call(
        forward_kernel,
        grid=(1,),
        in_specs=[SMEM, group_cols] + [pair] * len(blocks),
        out_specs=group_cols,
        out_shape=jax.ShapeDtypeStruct((tokens, width), jnp.bfloat16),
        scratch_shapes=[pltpu.VMEM((keys, tokens), jnp.float32)],
        compiler_params=pltpu.CompilerParams(vmem_limit_bytes=40 * 1024 * 1024),
        cost_estimate=pl.CostEstimate(
            flops=4 * tokens * keys * width, bytes_accessed=4 << 20, transcendentals=0
        ),
        name="forward",
    )(lengths, queries, *blocks)


def backward(lengths, queries, grads, blocks):
    tokens, width = queries.shape
    group_cols, pair = specs(tokens, STEP_GROUPS)
    keys = (REACH + 1) * tokens
    kinds = [jnp.float32] + [jnp.bfloat16] * (REACH - 1) + [jnp.float32]
    return pl.pallas_call(
        backward_kernel,
        grid=(KV_HEADS // STEP_GROUPS,),
        in_specs=[SMEM, group_cols, group_cols] + [pair] * len(blocks),
        out_specs=[group_cols] + [pair] * len(blocks),
        out_shape=[jax.ShapeDtypeStruct((tokens, width), jnp.bfloat16)]
        + [jax.ShapeDtypeStruct(blocks[0].shape, kind) for kind in kinds],
        scratch_shapes=[
            pltpu.VMEM((keys, tokens), jnp.float32),
        ],
        compiler_params=pltpu.CompilerParams(vmem_limit_bytes=40 * 1024 * 1024),
        cost_estimate=pl.CostEstimate(
            flops=10 * tokens * keys * width, bytes_accessed=8 << 20, transcendentals=0
        ),
        name="backward",
    )(lengths, queries, grads, *blocks)


def window_sends(own, previous):
    place = lax.axis_index("ctx") % ROW
    return [jnp.where(place + d < ROW, own, previous) for d in range(1, ROW)]


def gather_window(own, previous, sends):
    moved = [in_row(sent, d) for d, sent in enumerate(sends, 1)]
    return [previous] + moved[::-1] + [own]


def return_terms(terms):
    place = lax.axis_index("ctx") % ROW
    previous, own = terms[0], terms[REACH]
    for distance in range(1, ROW):
        back = in_row(terms[REACH - distance], -distance).astype(jnp.float32)
        here = place + distance < ROW
        own = own + jnp.where(here, back, 0.0)
        previous = previous + jnp.where(here, 0.0, back)
    crossed = across_rows(previous.astype(jnp.bfloat16), -ROW)
    return own, crossed


def body(
    sent_queries,
    sent_keyvals,
    forward_lengths,
    kept_queries,
    kept_keyvals,
    sent_grad,
    backward_lengths,
):
    kept = kept_keyvals[0].transpose(1, 0, 2)
    sent = sent_keyvals[0].transpose(1, 0, 2)
    kept_previous = across_rows(kept, ROW)
    grads = along_section(after(sent_grad[0], (kept_previous, sent)), -1)
    kept_sends = window_sends(kept, kept_previous)
    kept_window = gather_window(kept, kept_previous, kept_sends)
    sent, queries = after((sent, sent_queries[0]), kept_window[REACH - 1])
    arrived_previous = across_rows_and_section(sent, ROW)
    arrived = along_section(sent, 1)

    arrived_queries = along_section(queries, 1)
    results = backward(backward_lengths, kept_queries[0], grads, kept_window)
    own, crossed = return_terms(results[1:])
    arrived_window = gather_window(
        arrived, arrived_previous, window_sends(arrived, arrived_previous)
    )
    attention_out = forward(forward_lengths, arrived_queries, arrived_window)
    keyval_grad = (own + crossed.astype(jnp.float32)).astype(jnp.bfloat16).transpose(1, 0, 2)
    return attention_out[None], results[0][None], keyval_grad[None]


def solution(mesh):
    placed = (
        P("section", "ctx", None),
        P("section", "ctx", None, None),
        P("section", None),
        P("section", "ctx", None),
        P("section", "ctx", None, None),
        P("section", "ctx", None),
        P("section", None),
    )
    return jax.shard_map(
        body,
        mesh=mesh,
        in_specs=placed,
        out_specs=(
            P("section", "ctx", None),
            P("section", "ctx", None),
            P("section", "ctx", None, None),
        ),
        check_vma=False,
    )
```

```python
import math

import jax
import jax.numpy as jnp
from jax import lax
from jax.experimental import pallas as pl
from jax.experimental.pallas import tpu as pltpu
from jax.sharding import PartitionSpec as P

QUERY_HEADS = 32
KV_HEADS = 4
GROUP = QUERY_HEADS // KV_HEADS
WIDTH = 128
REACH = 4
ROW = 4
LOGIT_SCALE = 1.0 / math.sqrt(WIDTH)
EXP2_SCALE = LOGIT_SCALE * math.log2(math.e)
MASKED = -1e30
CHUNK_HEADS = 2
STEP_GROUPS = 2

SMEM = pl.BlockSpec(memory_space=pltpu.SMEM)


def along_section(block, distance):
    size = lax.axis_size("section")
    return lax.ppermute(
        block, "section", [(i, (i + distance) % size) for i in range(size)]
    )


def across_rows(block, distance):
    size = lax.axis_size("ctx")
    return lax.ppermute(
        block,
        "ctx",
        [(i, i + distance) for i in range(size) if 0 <= i + distance < size],
    )


def across_rows_and_section(block, distance):
    sections, size = lax.axis_size("section"), lax.axis_size("ctx")
    route = [
        (s * size + c, (s + 1) % sections * size + c + distance)
        for s in range(sections)
        for c in range(size)
        if 0 <= c + distance < size
    ]
    return lax.ppermute(block, ("section", "ctx"), route)


def in_row(block, distance):
    size = lax.axis_size("ctx")
    return lax.ppermute(
        block,
        "ctx",
        [(c, c // ROW * ROW + (c + distance) % ROW) for c in range(size)],
    )


def after(values, earlier):
    return lax.optimization_barrier((values, earlier))[0]


def nt_dot(a, b):
    return lax.dot_general(a, b, (((1,), (1,)), ((), ())), preferred_element_type=jnp.float32)


def nn_dot(a, b):
    return jnp.dot(a, b, preferred_element_type=jnp.float32)


def write_bias(lengths_ref, bias_ref):
    tokens = bias_ref.shape[1]
    first_row = lax.axis_index("ctx") * tokens
    query = first_row + lax.broadcasted_iota(jnp.int32, (1, tokens), 1)
    start = jnp.zeros((1, tokens), jnp.int32)
    end = jnp.int32(0)
    for k in range(lengths_ref.shape[1]):
        end = end + lengths_ref[0, k]
        start = jnp.where(query >= end, end, start)
    for b in range(REACH + 1):
        key = (
            first_row
            + (b - REACH) * tokens
            + lax.broadcasted_iota(jnp.int32, (tokens, tokens), 0)
        )
        allowed = (key >= start) & (key <= query)
        bias_ref[b * tokens : (b + 1) * tokens, :] = jnp.where(allowed, 0.0, MASKED)


def head_rows(ref, first, count):
    return jnp.concatenate(
        [ref[:, h * WIDTH : (h + 1) * WIDTH] for h in range(first, first + count)], axis=0
    )


def window(block_refs, index, group):
    columns = slice(group * WIDTH, (group + 1) * WIDTH)
    return jnp.concatenate([ref[index, :, columns] for ref in block_refs], axis=0)


def write_heads(ref, first, count, transposed):
    for k in range(count):
        at = (first + k) * WIDTH
        ref[:, at : at + WIDTH] = transposed[:, k * WIDTH : (k + 1) * WIDTH].T.astype(ref.dtype)


def exponentials(scores, bias):
    scores = scores * EXP2_SCALE + bias
    return jnp.exp2(scores - jnp.max(scores, axis=0, keepdims=True))


def forward_kernel(lengths_ref, q_ref, *refs):
    block_refs, (out_ref, bias_ref) = refs[: REACH + 1], refs[REACH + 1 :]
    write_bias(lengths_ref, bias_ref)
    bias = jnp.concatenate([bias_ref[...]] * GROUP, axis=1)
    for group in range(KV_HEADS):
        queries = head_rows(q_ref, group * GROUP, GROUP)
        e = exponentials(nt_dot(window(block_refs, 0, group), queries), bias)
        total = jnp.sum(e, axis=0, keepdims=True)
        out_t = nn_dot(window(block_refs, 1, group).T, e.astype(jnp.bfloat16)) / total
        write_heads(out_ref, group * GROUP, GROUP, out_t)


def backward_kernel(lengths_ref, q_ref, g_ref, *refs):
    block_refs, refs = refs[: REACH + 1], refs[REACH + 1 :]
    dq_ref, *grad_refs, bias_ref = refs
    tokens = q_ref.shape[0]

    @pl.when(pl.program_id(0) == 0)
    def _():
        write_bias(lengths_ref, bias_ref)

    bias = jnp.concatenate([bias_ref[...]] * CHUNK_HEADS, axis=1)
    keys = [window(block_refs, 0, group) for group in range(STEP_GROUPS)]
    values = [window(block_refs, 1, group) for group in range(STEP_GROUPS)]
    keys_t = [k.T for k in keys]
    chunks = [
        (group, group * GROUP + first)
        for group in range(STEP_GROUPS)
        for first in range(0, GROUP, CHUNK_HEADS)
    ]

    def products(chunk):
        group, first = chunk
        queries = head_rows(q_ref, first, CHUNK_HEADS)
        grads = head_rows(g_ref, first, CHUNK_HEADS)
        return queries, grads, nt_dot(keys[group], queries), nt_dot(values[group], grads)

    def score_terms(scores, prob_grad):
        e = exponentials(scores, bias)
        inverse = 1.0 / jnp.sum(e, axis=0, keepdims=True)
        delta = jnp.sum(e * prob_grad, axis=0, keepdims=True) * inverse
        probs = e * inverse
        return probs.astype(jnp.bfloat16), (probs * (prob_grad - delta)).astype(jnp.bfloat16)

    totals = [None] * STEP_GROUPS

    def gradients(chunk, queries, grads, probs, score_grad):
        group, first = chunk
        dq_t = nn_dot(keys_t[group], score_grad) * LOGIT_SCALE
        write_heads(dq_ref, first, CHUNK_HEADS, dq_t)
        terms = (nn_dot(score_grad, queries), nn_dot(probs, grads))
        if totals[group] is not None:
            terms = tuple(a + b for a, b in zip(totals[group], terms))
        totals[group] = terms

    ready, waiting = products(chunks[0]), None
    for at, chunk in enumerate(chunks):
        upcoming = products(chunks[at + 1]) if at + 1 < len(chunks) else None
        queries, grads, scores, prob_grad = ready
        terms = score_terms(scores, prob_grad)
        if waiting is not None:
            gradients(*waiting)
        ready, waiting = upcoming, (chunk, queries, grads, *terms)
    gradients(*waiting)

    for group, (key_grad, value_grad) in enumerate(totals):
        columns = slice(group * WIDTH, (group + 1) * WIDTH)
        for b, ref in enumerate(grad_refs):
            rows = slice(b * tokens, (b + 1) * tokens)
            ref[0, :, columns] = (key_grad[rows] * LOGIT_SCALE).astype(ref.dtype)
            ref[1, :, columns] = value_grad[rows].astype(ref.dtype)


def specs(tokens, groups):
    group_cols = pl.BlockSpec((tokens, groups * GROUP * WIDTH), lambda g: (0, g))
    pair = pl.BlockSpec((2, tokens, groups * WIDTH), lambda g: (0, 0, g))
    return group_cols, pair


def forward(lengths, queries, blocks):
    tokens, width = queries.shape
    group_cols, pair = specs(tokens, KV_HEADS)
    keys = (REACH + 1) * tokens
    return pl.pallas_call(
        forward_kernel,
        grid=(1,),
        in_specs=[SMEM, group_cols] + [pair] * len(blocks),
        out_specs=group_cols,
        out_shape=jax.ShapeDtypeStruct((tokens, width), jnp.bfloat16),
        scratch_shapes=[pltpu.VMEM((keys, tokens), jnp.float32)],
        compiler_params=pltpu.CompilerParams(vmem_limit_bytes=40 * 1024 * 1024),
        cost_estimate=pl.CostEstimate(
            flops=4 * tokens * keys * width, bytes_accessed=4 << 20, transcendentals=0
        ),
        name="forward",
    )(lengths, queries, *blocks)


def backward(lengths, queries, grads, blocks):
    tokens, width = queries.shape
    group_cols, pair = specs(tokens, STEP_GROUPS)
    keys = (REACH + 1) * tokens
    kinds = [jnp.float32] + [jnp.bfloat16] * (REACH - 1) + [jnp.float32]
    return pl.pallas_call(
        backward_kernel,
        grid=(KV_HEADS // STEP_GROUPS,),
        in_specs=[SMEM, group_cols, group_cols] + [pair] * len(blocks),
        out_specs=[group_cols] + [pair] * len(blocks),
        out_shape=[jax.ShapeDtypeStruct((tokens, width), jnp.bfloat16)]
        + [jax.ShapeDtypeStruct(blocks[0].shape, kind) for kind in kinds],
        scratch_shapes=[
            pltpu.VMEM((keys, tokens), jnp.float32),
        ],
        compiler_params=pltpu.CompilerParams(vmem_limit_bytes=40 * 1024 * 1024),
        cost_estimate=pl.CostEstimate(
            flops=10 * tokens * keys * width, bytes_accessed=8 << 20, transcendentals=0
        ),
        name="backward",
    )(lengths, queries, grads, *blocks)


def window_sends(own, previous):
    place = lax.axis_index("ctx") % ROW
    return [jnp.where(place + d < ROW, own, previous) for d in range(1, ROW)]


def gather_window(own, previous, sends):
    moved = [in_row(sent, d) for d, sent in enumerate(sends, 1)]
    return [previous] + moved[::-1] + [own]


def return_terms(terms):
    place = lax.axis_index("ctx") % ROW
    previous, own = terms[0], terms[REACH]
    for distance in range(1, ROW):
        back = in_row(terms[REACH - distance], -distance).astype(jnp.float32)
        here = place + distance < ROW
        own = own + jnp.where(here, back, 0.0)
        previous = previous + jnp.where(here, 0.0, back)
    crossed = across_rows(previous.astype(jnp.bfloat16), -ROW)
    return own, crossed


def body(
    sent_queries,
    sent_keyvals,
    forward_lengths,
    kept_queries,
    kept_keyvals,
    sent_grad,
    backward_lengths,
):
    kept = kept_keyvals[0].transpose(1, 0, 2)
    sent = after(sent_keyvals[0], kept).transpose(1, 0, 2)
    kept_previous = across_rows(kept, ROW)
    arrived = along_section(sent, 1)
    kept_previous = after(kept_previous, arrived)
    grads = along_section(after(sent_grad[0], (kept_previous, sent)), -1)
    kept_sends = window_sends(kept, kept_previous)
    kept_window = gather_window(kept, kept_previous, kept_sends)
    sent = after(sent, kept_window[REACH - 1])
    arrived_previous = across_rows_and_section(sent, ROW)

    results = backward(backward_lengths, kept_queries[0], grads, kept_window)
    terms = after(results[1:], (arrived_previous, arrived))
    queries = after(sent_queries[0], terms[0])
    arrived_queries = along_section(queries, 1)
    arrived_sends = window_sends(arrived, arrived_previous)
    own, crossed = return_terms(terms)
    arrived_window = gather_window(arrived, arrived_previous, arrived_sends)
    attention_out = forward(forward_lengths, arrived_queries, arrived_window)
    crossed = after(crossed, attention_out)
    keyval_grad = (own + crossed.astype(jnp.float32)).astype(jnp.bfloat16).transpose(1, 0, 2)
    return attention_out[None], results[0][None], keyval_grad[None]


def solution(mesh):
    placed = (
        P("section", "ctx", None),
        P("section", "ctx", None, None),
        P("section", None),
        P("section", "ctx", None),
        P("section", "ctx", None, None),
        P("section", "ctx", None),
        P("section", None),
    )
    return jax.shard_map(
        body,
        mesh=mesh,
        in_specs=placed,
        out_specs=(
            P("section", "ctx", None),
            P("section", "ctx", None),
            P("section", "ctx", None, None),
        ),
        check_vma=False,
    )
```

```python
import math

import jax
import jax.numpy as jnp
from jax import lax
from jax.experimental import pallas as pl
from jax.experimental.pallas import tpu as pltpu
from jax.sharding import PartitionSpec as P

QUERY_HEADS = 32
KV_HEADS = 4
GROUP = QUERY_HEADS // KV_HEADS
WIDTH = 128
REACH = 4
ROW = 4
LOGIT_SCALE = 1.0 / math.sqrt(WIDTH)
EXP2_SCALE = LOGIT_SCALE * math.log2(math.e)
MASKED = -1e30
CHUNK_HEADS = 2
STEP_GROUPS = 2

SMEM = pl.BlockSpec(memory_space=pltpu.SMEM)


def along_section(block, distance):
    size = lax.axis_size("section")
    return lax.ppermute(
        block, "section", [(i, (i + distance) % size) for i in range(size)]
    )


def across_rows(block, distance):
    size = lax.axis_size("ctx")
    return lax.ppermute(
        block,
        "ctx",
        [(i, i + distance) for i in range(size) if 0 <= i + distance < size],
    )


def across_rows_and_section(block, distance):
    sections, size = lax.axis_size("section"), lax.axis_size("ctx")
    route = [
        (s * size + c, (s + 1) % sections * size + c + distance)
        for s in range(sections)
        for c in range(size)
        if 0 <= c + distance < size
    ]
    return lax.ppermute(block, ("section", "ctx"), route)


def in_row(block, distance):
    size = lax.axis_size("ctx")
    return lax.ppermute(
        block,
        "ctx",
        [(c, c // ROW * ROW + (c + distance) % ROW) for c in range(size)],
    )


def after(values, earlier):
    return lax.optimization_barrier((values, earlier))[0]


def nt_dot(a, b):
    return lax.dot_general(a, b, (((1,), (1,)), ((), ())), preferred_element_type=jnp.float32)


def nn_dot(a, b):
    return jnp.dot(a, b, preferred_element_type=jnp.float32)


def write_bias(lengths_ref, bias_ref):
    tokens = bias_ref.shape[1]
    first_row = lax.axis_index("ctx") * tokens
    query = first_row + lax.broadcasted_iota(jnp.int32, (1, tokens), 1)
    start = jnp.zeros((1, tokens), jnp.int32)
    end = jnp.int32(0)
    for k in range(lengths_ref.shape[1]):
        end = end + lengths_ref[0, k]
        start = jnp.where(query >= end, end, start)
    for b in range(REACH + 1):
        key = (
            first_row
            + (b - REACH) * tokens
            + lax.broadcasted_iota(jnp.int32, (tokens, tokens), 0)
        )
        allowed = (key >= start) & (key <= query)
        bias_ref[b * tokens : (b + 1) * tokens, :] = jnp.where(allowed, 0.0, MASKED)


def head_rows(ref, first, count):
    return jnp.concatenate(
        [ref[:, h * WIDTH : (h + 1) * WIDTH] for h in range(first, first + count)], axis=0
    )


def window(block_refs, index, group):
    columns = slice(group * WIDTH, (group + 1) * WIDTH)
    return jnp.concatenate([ref[index, :, columns] for ref in block_refs], axis=0)


def write_heads(ref, first, count, transposed):
    for k in range(count):
        at = (first + k) * WIDTH
        ref[:, at : at + WIDTH] = transposed[:, k * WIDTH : (k + 1) * WIDTH].T.astype(ref.dtype)


def exponentials(scores, bias):
    scores = scores * EXP2_SCALE + bias
    return jnp.exp2(scores - jnp.max(scores, axis=0, keepdims=True))


def forward_kernel(lengths_ref, q_ref, *refs):
    block_refs, (out_ref, bias_ref) = refs[: REACH + 1], refs[REACH + 1 :]
    write_bias(lengths_ref, bias_ref)
    bias = jnp.concatenate([bias_ref[...]] * GROUP, axis=1)
    for group in range(KV_HEADS):
        queries = head_rows(q_ref, group * GROUP, GROUP)
        e = exponentials(nt_dot(window(block_refs, 0, group), queries), bias)
        total = jnp.sum(e, axis=0, keepdims=True)
        out_t = nn_dot(window(block_refs, 1, group).T, e.astype(jnp.bfloat16)) / total
        write_heads(out_ref, group * GROUP, GROUP, out_t)


def backward_kernel(lengths_ref, q_ref, g_ref, *refs):
    block_refs, refs = refs[: REACH + 1], refs[REACH + 1 :]
    dq_ref, *grad_refs, bias_ref = refs
    tokens = q_ref.shape[0]

    @pl.when(pl.program_id(0) == 0)
    def _():
        write_bias(lengths_ref, bias_ref)

    bias = jnp.concatenate([bias_ref[...]] * CHUNK_HEADS, axis=1)
    keys = [window(block_refs, 0, group) for group in range(STEP_GROUPS)]
    values = [window(block_refs, 1, group) for group in range(STEP_GROUPS)]
    keys_t = [k.T for k in keys]
    chunks = [
        (group, group * GROUP + first)
        for group in range(STEP_GROUPS)
        for first in range(0, GROUP, CHUNK_HEADS)
    ]

    def products(chunk):
        group, first = chunk
        queries = head_rows(q_ref, first, CHUNK_HEADS)
        grads = head_rows(g_ref, first, CHUNK_HEADS)
        return queries, grads, nt_dot(keys[group], queries), nt_dot(values[group], grads)

    def score_terms(scores, prob_grad):
        e = exponentials(scores, bias)
        inverse = 1.0 / jnp.sum(e, axis=0, keepdims=True)
        delta = jnp.sum(e * prob_grad, axis=0, keepdims=True) * inverse
        probs = e * inverse
        rounded = probs.astype(jnp.bfloat16)
        return rounded, rounded * (prob_grad - delta).astype(jnp.bfloat16)

    totals = [None] * STEP_GROUPS

    def gradients(chunk, queries, grads, probs, score_grad):
        group, first = chunk
        dq_t = nn_dot(keys_t[group], score_grad) * LOGIT_SCALE
        write_heads(dq_ref, first, CHUNK_HEADS, dq_t)
        terms = (nn_dot(score_grad, queries), nn_dot(probs, grads))
        if totals[group] is not None:
            terms = tuple(a + b for a, b in zip(totals[group], terms))
        totals[group] = terms

    ready, waiting = products(chunks[0]), None
    for at, chunk in enumerate(chunks):
        upcoming = products(chunks[at + 1]) if at + 1 < len(chunks) else None
        queries, grads, scores, prob_grad = ready
        terms = score_terms(scores, prob_grad)
        if waiting is not None:
            gradients(*waiting)
        ready, waiting = upcoming, (chunk, queries, grads, *terms)
    gradients(*waiting)

    for group, (key_grad, value_grad) in enumerate(totals):
        columns = slice(group * WIDTH, (group + 1) * WIDTH)
        for b, ref in enumerate(grad_refs):
            rows = slice(b * tokens, (b + 1) * tokens)
            ref[0, :, columns] = (key_grad[rows] * LOGIT_SCALE).astype(ref.dtype)
            ref[1, :, columns] = value_grad[rows].astype(ref.dtype)


def specs(tokens, groups):
    group_cols = pl.BlockSpec((tokens, groups * GROUP * WIDTH), lambda g: (0, g))
    pair = pl.BlockSpec((2, tokens, groups * WIDTH), lambda g: (0, 0, g))
    return group_cols, pair


def forward(lengths, queries, blocks):
    tokens, width = queries.shape
    group_cols, pair = specs(tokens, KV_HEADS)
    keys = (REACH + 1) * tokens
    return pl.pallas_call(
        forward_kernel,
        grid=(1,),
        in_specs=[SMEM, group_cols] + [pair] * len(blocks),
        out_specs=group_cols,
        out_shape=jax.ShapeDtypeStruct((tokens, width), jnp.bfloat16),
        scratch_shapes=[pltpu.VMEM((keys, tokens), jnp.float32)],
        compiler_params=pltpu.CompilerParams(vmem_limit_bytes=40 * 1024 * 1024),
        cost_estimate=pl.CostEstimate(
            flops=4 * tokens * keys * width, bytes_accessed=4 << 20, transcendentals=0
        ),
        name="forward",
    )(lengths, queries, *blocks)


def backward(lengths, queries, grads, blocks):
    tokens, width = queries.shape
    group_cols, pair = specs(tokens, STEP_GROUPS)
    keys = (REACH + 1) * tokens
    kinds = [jnp.float32] + [jnp.bfloat16] * (REACH - 1) + [jnp.float32]
    return pl.pallas_call(
        backward_kernel,
        grid=(KV_HEADS // STEP_GROUPS,),
        in_specs=[SMEM, group_cols, group_cols] + [pair] * len(blocks),
        out_specs=[group_cols] + [pair] * len(blocks),
        out_shape=[jax.ShapeDtypeStruct((tokens, width), jnp.bfloat16)]
        + [jax.ShapeDtypeStruct(blocks[0].shape, kind) for kind in kinds],
        scratch_shapes=[
            pltpu.VMEM((keys, tokens), jnp.float32),
        ],
        compiler_params=pltpu.CompilerParams(vmem_limit_bytes=40 * 1024 * 1024),
        cost_estimate=pl.CostEstimate(
            flops=10 * tokens * keys * width, bytes_accessed=8 << 20, transcendentals=0
        ),
        name="backward",
    )(lengths, queries, grads, *blocks)


def window_sends(own, previous):
    place = lax.axis_index("ctx") % ROW
    return [jnp.where(place + d < ROW, own, previous) for d in range(1, ROW)]


def gather_window(own, previous, sends):
    moved = [in_row(sent, d) for d, sent in enumerate(sends, 1)]
    return [previous] + moved[::-1] + [own]


def return_terms(terms):
    place = lax.axis_index("ctx") % ROW
    previous, own = terms[0], terms[REACH]
    for distance in range(1, ROW):
        back = in_row(terms[REACH - distance], -distance).astype(jnp.float32)
        here = place + distance < ROW
        own = own + jnp.where(here, back, 0.0)
        previous = previous + jnp.where(here, 0.0, back)
    crossed = across_rows(previous.astype(jnp.bfloat16), -ROW)
    return own, crossed


def body(
    sent_queries,
    sent_keyvals,
    forward_lengths,
    kept_queries,
    kept_keyvals,
    sent_grad,
    backward_lengths,
):
    kept = kept_keyvals[0].transpose(1, 0, 2)
    sent = after(sent_keyvals[0], kept).transpose(1, 0, 2)
    kept_previous = across_rows(kept, ROW)
    arrived = along_section(sent, 1)
    kept_previous = after(kept_previous, arrived)
    kept_sends = window_sends(kept, kept_previous)
    grads = along_section(after(sent_grad[0], kept_sends), -1)
    kept_window = gather_window(kept, kept_previous, kept_sends)
    sent = after(sent, kept_window[REACH - 1])
    arrived_previous = across_rows_and_section(sent, ROW)

    results = backward(backward_lengths, kept_queries[0], grads, kept_window)
    terms = after(results[1:], (arrived_previous, arrived))
    queries = after(sent_queries[0], terms[0])
    arrived_queries = along_section(queries, 1)
    arrived_sends = window_sends(arrived, arrived_previous)
    own, crossed = return_terms(terms)
    arrived_window = gather_window(arrived, arrived_previous, arrived_sends)
    attention_out = forward(forward_lengths, arrived_queries, arrived_window)
    crossed = after(crossed, attention_out)
    keyval_grad = (own + crossed.astype(jnp.float32)).astype(jnp.bfloat16).transpose(1, 0, 2)
    return attention_out[None], results[0][None], keyval_grad[None]


def solution(mesh):
    placed = (
        P("section", "ctx", None),
        P("section", "ctx", None, None),
        P("section", None),
        P("section", "ctx", None),
        P("section", "ctx", None, None),
        P("section", "ctx", None),
        P("section", None),
    )
    return jax.shard_map(
        body,
        mesh=mesh,
        in_specs=placed,
        out_specs=(
            P("section", "ctx", None),
            P("section", "ctx", None),
            P("section", "ctx", None, None),
        ),
        check_vma=False,
    )
```

```python
import math

import jax
import jax.numpy as jnp
from jax import lax
from jax.experimental import pallas as pl
from jax.experimental.pallas import tpu as pltpu
from jax.sharding import PartitionSpec as P

QUERY_HEADS = 32
KV_HEADS = 4
GROUP = QUERY_HEADS // KV_HEADS
WIDTH = 128
REACH = 4
ROW = 4
LOGIT_SCALE = 1.0 / math.sqrt(WIDTH)
EXP2_SCALE = LOGIT_SCALE * math.log2(math.e)
MASKED = -1e30
CHUNK_HEADS = 2
STEP_GROUPS = 2

SMEM = pl.BlockSpec(memory_space=pltpu.SMEM)


def along_section(block, distance):
    size = lax.axis_size("section")
    return lax.ppermute(
        block, "section", [(i, (i + distance) % size) for i in range(size)]
    )


def across_rows(block, distance):
    size = lax.axis_size("ctx")
    return lax.ppermute(
        block,
        "ctx",
        [(i, i + distance) for i in range(size) if 0 <= i + distance < size],
    )


def across_rows_and_section(block, distance):
    sections, size = lax.axis_size("section"), lax.axis_size("ctx")
    route = [
        (s * size + c, (s + 1) % sections * size + c + distance)
        for s in range(sections)
        for c in range(size)
        if 0 <= c + distance < size
    ]
    return lax.ppermute(block, ("section", "ctx"), route)


def in_row(block, distance):
    size = lax.axis_size("ctx")
    return lax.ppermute(
        block,
        "ctx",
        [(c, c // ROW * ROW + (c + distance) % ROW) for c in range(size)],
    )


def after(values, earlier):
    return lax.optimization_barrier((values, earlier))[0]


def nt_dot(a, b):
    return lax.dot_general(a, b, (((1,), (1,)), ((), ())), preferred_element_type=jnp.float32)


def nn_dot(a, b):
    return jnp.dot(a, b, preferred_element_type=jnp.float32)


def write_bias(lengths_ref, bias_ref):
    tokens = bias_ref.shape[1]
    first_row = lax.axis_index("ctx") * tokens
    query = first_row + lax.broadcasted_iota(jnp.int32, (1, tokens), 1)
    start = jnp.zeros((1, tokens), jnp.int32)
    end = jnp.int32(0)
    for k in range(lengths_ref.shape[1]):
        end = end + lengths_ref[0, k]
        start = jnp.where(query >= end, end, start)
    for b in range(REACH + 1):
        key = (
            first_row
            + (b - REACH) * tokens
            + lax.broadcasted_iota(jnp.int32, (tokens, tokens), 0)
        )
        allowed = (key >= start) & (key <= query)
        bias_ref[b * tokens : (b + 1) * tokens, :] = jnp.where(allowed, 0.0, MASKED)


def head_rows(ref, first, count):
    return jnp.concatenate(
        [ref[:, h * WIDTH : (h + 1) * WIDTH] for h in range(first, first + count)], axis=0
    )


def window(block_refs, index, group):
    columns = slice(group * WIDTH, (group + 1) * WIDTH)
    return jnp.concatenate([ref[index, :, columns] for ref in block_refs], axis=0)


def write_heads(ref, first, count, transposed):
    for k in range(count):
        at = (first + k) * WIDTH
        ref[:, at : at + WIDTH] = transposed[:, k * WIDTH : (k + 1) * WIDTH].T.astype(ref.dtype)


def exponentials(scores, bias):
    scores = scores * EXP2_SCALE + bias
    return jnp.exp2(scores - jnp.max(scores, axis=0, keepdims=True))


def forward_kernel(lengths_ref, q_ref, *refs):
    block_refs, (out_ref, bias_ref) = refs[: REACH + 1], refs[REACH + 1 :]
    write_bias(lengths_ref, bias_ref)
    bias = jnp.concatenate([bias_ref[...]] * GROUP, axis=1)

    def group_scores(group):
        return nt_dot(window(block_refs, 0, group), head_rows(q_ref, group * GROUP, GROUP))

    scores = group_scores(0)
    for group in range(KV_HEADS):
        upcoming = group_scores(group + 1) if group + 1 < KV_HEADS else None
        e = exponentials(scores, bias)
        total = jnp.sum(e, axis=0, keepdims=True)
        out_t = nn_dot(window(block_refs, 1, group).T, e.astype(jnp.bfloat16)) / total
        write_heads(out_ref, group * GROUP, GROUP, out_t)
        scores = upcoming


def backward_kernel(lengths_ref, q_ref, g_ref, *refs):
    block_refs, refs = refs[: REACH + 1], refs[REACH + 1 :]
    dq_ref, *grad_refs, bias_ref = refs
    tokens = q_ref.shape[0]

    @pl.when(pl.program_id(0) == 0)
    def _():
        write_bias(lengths_ref, bias_ref)

    bias = jnp.concatenate([bias_ref[...]] * CHUNK_HEADS, axis=1)
    keys = [window(block_refs, 0, group) for group in range(STEP_GROUPS)]
    values = [window(block_refs, 1, group) for group in range(STEP_GROUPS)]
    keys_t = [k.T for k in keys]
    chunks = [
        (group, group * GROUP + first)
        for group in range(STEP_GROUPS)
        for first in range(0, GROUP, CHUNK_HEADS)
    ]

    def products(chunk):
        group, first = chunk
        queries = head_rows(q_ref, first, CHUNK_HEADS)
        grads = head_rows(g_ref, first, CHUNK_HEADS)
        return queries, grads, nt_dot(keys[group], queries), nt_dot(values[group], grads)

    def score_terms(scores, prob_grad):
        e = exponentials(scores, bias)
        inverse = 1.0 / jnp.sum(e, axis=0, keepdims=True)
        delta = jnp.sum(e * prob_grad, axis=0, keepdims=True) * inverse
        probs = e * inverse
        rounded = probs.astype(jnp.bfloat16)
        return rounded, rounded * (prob_grad - delta).astype(jnp.bfloat16)

    totals = [None] * STEP_GROUPS

    def gradients(chunk, queries, grads, probs, score_grad):
        group, first = chunk
        dq_t = nn_dot(keys_t[group], score_grad) * LOGIT_SCALE
        write_heads(dq_ref, first, CHUNK_HEADS, dq_t)
        terms = (nn_dot(score_grad, queries), nn_dot(probs, grads))
        if totals[group] is not None:
            terms = tuple(a + b for a, b in zip(totals[group], terms))
        totals[group] = terms

    ready, waiting = products(chunks[0]), None
    for at, chunk in enumerate(chunks):
        upcoming = products(chunks[at + 1]) if at + 1 < len(chunks) else None
        queries, grads, scores, prob_grad = ready
        terms = score_terms(scores, prob_grad)
        if waiting is not None:
            gradients(*waiting)
        ready, waiting = upcoming, (chunk, queries, grads, *terms)
    gradients(*waiting)

    for group, (key_grad, value_grad) in enumerate(totals):
        columns = slice(group * WIDTH, (group + 1) * WIDTH)
        for b, ref in enumerate(grad_refs):
            rows = slice(b * tokens, (b + 1) * tokens)
            ref[0, :, columns] = (key_grad[rows] * LOGIT_SCALE).astype(ref.dtype)
            ref[1, :, columns] = value_grad[rows].astype(ref.dtype)


def specs(tokens, groups):
    group_cols = pl.BlockSpec((tokens, groups * GROUP * WIDTH), lambda g: (0, g))
    pair = pl.BlockSpec((2, tokens, groups * WIDTH), lambda g: (0, 0, g))
    return group_cols, pair


def forward(lengths, queries, blocks):
    tokens, width = queries.shape
    group_cols, pair = specs(tokens, KV_HEADS)
    keys = (REACH + 1) * tokens
    return pl.pallas_call(
        forward_kernel,
        grid=(1,),
        in_specs=[SMEM, group_cols] + [pair] * len(blocks),
        out_specs=group_cols,
        out_shape=jax.ShapeDtypeStruct((tokens, width), jnp.bfloat16),
        scratch_shapes=[pltpu.VMEM((keys, tokens), jnp.float32)],
        compiler_params=pltpu.CompilerParams(vmem_limit_bytes=40 * 1024 * 1024),
        cost_estimate=pl.CostEstimate(
            flops=4 * tokens * keys * width, bytes_accessed=4 << 20, transcendentals=0
        ),
        name="forward",
    )(lengths, queries, *blocks)


def backward(lengths, queries, grads, blocks):
    tokens, width = queries.shape
    group_cols, pair = specs(tokens, STEP_GROUPS)
    keys = (REACH + 1) * tokens
    kinds = [jnp.float32] + [jnp.bfloat16] * (REACH - 1) + [jnp.float32]
    return pl.pallas_call(
        backward_kernel,
        grid=(KV_HEADS // STEP_GROUPS,),
        in_specs=[SMEM, group_cols, group_cols] + [pair] * len(blocks),
        out_specs=[group_cols] + [pair] * len(blocks),
        out_shape=[jax.ShapeDtypeStruct((tokens, width), jnp.bfloat16)]
        + [jax.ShapeDtypeStruct(blocks[0].shape, kind) for kind in kinds],
        scratch_shapes=[
            pltpu.VMEM((keys, tokens), jnp.float32),
        ],
        compiler_params=pltpu.CompilerParams(vmem_limit_bytes=40 * 1024 * 1024),
        cost_estimate=pl.CostEstimate(
            flops=10 * tokens * keys * width, bytes_accessed=8 << 20, transcendentals=0
        ),
        name="backward",
    )(lengths, queries, grads, *blocks)


def window_sends(own, previous):
    place = lax.axis_index("ctx") % ROW
    return [jnp.where(place + d < ROW, own, previous) for d in range(1, ROW)]


def gather_window(own, previous, sends):
    moved = [in_row(sent, d) for d, sent in enumerate(sends, 1)]
    return [previous] + moved[::-1] + [own]


def return_terms(terms):
    place = lax.axis_index("ctx") % ROW
    previous, own = terms[0], terms[REACH]
    for distance in range(1, ROW):
        back = in_row(terms[REACH - distance], -distance).astype(jnp.float32)
        here = place + distance < ROW
        own = own + jnp.where(here, back, 0.0)
        previous = previous + jnp.where(here, 0.0, back)
    crossed = across_rows(previous.astype(jnp.bfloat16), -ROW)
    return own, crossed


def body(
    sent_queries,
    sent_keyvals,
    forward_lengths,
    kept_queries,
    kept_keyvals,
    sent_grad,
    backward_lengths,
):
    kept = kept_keyvals[0].transpose(1, 0, 2)
    sent = after(sent_keyvals[0], kept).transpose(1, 0, 2)
    kept_previous = across_rows(kept, ROW)
    arrived = along_section(sent, 1)
    kept_previous = after(kept_previous, arrived)
    kept_sends = window_sends(kept, kept_previous)
    grads = along_section(after(sent_grad[0], kept_sends), -1)
    kept_window = gather_window(kept, kept_previous, kept_sends)
    sent = after(sent, kept_window[REACH - 1])
    arrived_previous = across_rows_and_section(sent, ROW)

    results = backward(backward_lengths, kept_queries[0], grads, kept_window)
    terms = after(results[1:], (arrived_previous, arrived))
    queries = after(sent_queries[0], terms[0])
    arrived_queries = along_section(queries, 1)
    arrived_sends = window_sends(arrived, arrived_previous)
    own, crossed = return_terms(terms)
    arrived_window = gather_window(arrived, arrived_previous, arrived_sends)
    attention_out = forward(forward_lengths, arrived_queries, arrived_window)
    crossed = after(crossed, attention_out)
    keyval_grad = (own + crossed.astype(jnp.float32)).astype(jnp.bfloat16).transpose(1, 0, 2)
    return attention_out[None], results[0][None], keyval_grad[None]


def solution(mesh):
    placed = (
        P("section", "ctx", None),
        P("section", "ctx", None, None),
        P("section", None),
        P("section", "ctx", None),
        P("section", "ctx", None, None),
        P("section", "ctx", None),
        P("section", None),
    )
    return jax.shard_map(
        body,
        mesh=mesh,
        in_specs=placed,
        out_specs=(
            P("section", "ctx", None),
            P("section", "ctx", None),
            P("section", "ctx", None, None),
        ),
        check_vma=False,
    )
```
